256 devices in a mesh: seq: 32 (over y, z), head: 8 (over x, core).
Axes of the slice: x: 4, y: 4, z: 8, core: 2. Of those that a mesh axis runs over, the one named last changes fastest.
Arguments:
- queries: float32 [8192, 2048], P('seq', 'head'), may hold values from -6 to 6
- reflect_keys: float32 [8192, 2, 2048], P('seq', None, 'head'), may hold values from -6 to 6
- reflect_values: float32 [8192, 2, 2048], P('seq', None, 'head'), may hold values from -0.625 to 0.625
- beta_logit: float32 [2, 16, 8192], P(None, 'head', 'seq'), may hold values from -1.5 to 6, as said below
- out_weight: bfloat16 [2048, 2048], P('head'), may hold values from -0.125 to 0.125
- out_grad: bfloat16 [8192, 2048], P('seq', 'head'), may hold values from -0.125 to 0.125
Outputs:
- output: bfloat16 [8192, 2048], P('seq', 'head')
- query_grad: float32 [8192, 2048], P('seq', 'head')
- key_grad: float32 [8192, 2, 2048], P('seq', None, 'head')
- value_grad: float32 [8192, 2, 2048], P('seq', None, 'head')
- logit_grad: float32 [2, 16, 8192], P(None, 'head', 'seq')
- weight_grad: float32 [2048, 2048], P(('head', 'seq'))
The draws below stay inside these ranges and needn't reach their ends.
Inputs may be any that keep to these rules, and one draw needn't show every extreme that they name: `beta_logit`: logits of the reflections' strengths.
All inputs are finite; a program needn't handle non-finite values.
Results may differ from the reference program's by a relative error of at most 0.02.
Values may be sent and summed in bfloat16 or wider, within the bound.
No kernel may reach another device: no remote copies, remote signals or barrier semaphores. Data moves between devices by JAX's collectives and lax.ppermute only.
A program may use at most 128 MiB of HBM per device.

```python
import jax
import jax.numpy as jnp
from jax import lax

HEADS = 16
HEAD_DIM = 128
D = 2048
BLOCK = 64
TOKENS = 8192


def draw_beta_logit(key, part):
    key_order = jax.random.fold_in(key, 11)
    key_slow = jax.random.fold_in(key, 12)
    key_quick = jax.random.fold_in(key, 13)
    order = jax.random.permutation(key_order, HEADS)
    slow_heads = (order < HEADS // 2).astype(jnp.float32)[None, :, None]
    slow_values = jax.random.uniform(key_slow, (2, HEADS, TOKENS), jnp.float32, 5.0, 6.0)
    quick_values = jax.random.uniform(key_quick, (2, HEADS, TOKENS), jnp.float32, -1.5, 1.5)
    return slow_heads * slow_values + (1.0 - slow_heads) * quick_values


def block_levels(key, shape, cuts, least, largest):
    level = 1.0
    for dim, parts in cuts:
        steps = jax.random.uniform(jax.random.fold_in(jax.random.fold_in(key, 6), dim), (parts,), jnp.float32, least / len(cuts), largest / len(cuts))
        level = level * jnp.repeat(jnp.exp(steps), shape[dim] // parts).reshape((-1,) + (1,) * (len(shape) - 1 - dim))
    return level


def bell_draw(stream_key, shape, deviation, reach, split=(), held_as=jnp.bfloat16):
    factor_of = block_levels(stream_key, shape, split, -0.22, 0.18) if split else 1.0
    drawn = jax.random.normal(stream_key, shape, jnp.float32) * deviation * factor_of
    return jnp.minimum(jnp.maximum(drawn, -reach), reach).astype(held_as)


def setup_inputs(seed: int = 0) -> dict:
    keys = jax.random.split(jax.random.key(seed), 7)
    queries = bell_draw(keys[0], (TOKENS, D), 1.0, 6.0, ((0, 32), (1, 8)), jnp.float32)
    reflect_keys = bell_draw(keys[1], (TOKENS, 2, D), 1.0, 6.0, ((0, 32), (2, 8)), jnp.float32)
    reflect_values = bell_draw(keys[2], (TOKENS, 2, D), 0.1, 0.625, ((0, 32), (2, 8)), jnp.float32)
    beta_logit = draw_beta_logit(jax.random.fold_in(keys[6], 71), 0)
    out_weight = bell_draw(keys[4], (D, D), D ** -0.5, 0.125, ((0, 8),))
    out_grad = bell_draw(keys[5], (TOKENS, D), 0.02, 0.125, ((0, 32), (1, 8)))
    return {"queries": queries, "reflect_keys": reflect_keys, "reflect_values": reflect_values, "beta_logit": beta_logit, "out_weight": out_weight, "out_grad": out_grad}


HIGHEST_PRECISION = lax.Precision.HIGHEST

def normalize(vectors):
    return vectors * lax.rsqrt(lax.optimization_barrier(jnp.sum(vectors * vectors, axis=-1, keepdims=True)) + 1e-06)

def block_core(carry_state, query_block, key_block, value_block, beta_block):
    pseudo = key_block.shape[1]
    width = key_block.shape[2]
    reflections = pseudo // query_block.shape[1]
    gram = jnp.einsum('hik,hjk->hij', key_block, key_block, precision=HIGHEST_PRECISION)
    row_index = jnp.arange(pseudo)[:, None]
    col_index = jnp.arange(pseudo)[None, :]
    system = jnp.where(col_index < row_index, gram, 0.0) * beta_block[:, :, None] + jnp.eye(pseudo, dtype=key_block.dtype)
    right_side = jnp.concatenate([key_block, value_block], axis=-1) * beta_block[:, :, None]
    solved = lax.linalg.triangular_solve(system, right_side, left_side=True, lower=True, unit_diagonal=True)
    key_weights = solved[:, :, :width]
    new_values = solved[:, :, width:] - jnp.einsum('hnk,hvk->hnv', key_weights, carry_state, precision=HIGHEST_PRECISION)
    scores = jnp.einsum('hck,hnk->hcn', query_block, key_block, precision=HIGHEST_PRECISION)
    visible = jnp.arange(pseudo)[None, :] <= reflections * jnp.arange(query_block.shape[1])[:, None] + reflections - 1
    scores = jnp.where(visible, scores, 0.0)
    mixed_block = jnp.einsum('hvk,hck->hcv', carry_state, query_block, precision=HIGHEST_PRECISION)
    mixed_block = mixed_block + jnp.einsum('hcn,hnv->hcv', scores, new_values, precision=HIGHEST_PRECISION)
    next_state = carry_state + jnp.einsum('hnv,hnk->hvk', new_values, key_block, precision=HIGHEST_PRECISION)
    return (mixed_block, next_state, key_weights)

def arrange(queries, reflect_keys, reflect_values, beta_logit, head_count):
    tokens_here = queries.shape[0]
    reflections = reflect_keys.shape[1]
    width = queries.shape[1] // head_count
    query_heads = normalize(queries.reshape(tokens_here, head_count, width)).transpose(1, 0, 2)
    key_heads = normalize(reflect_keys.reshape(tokens_here, reflections, head_count, width))
    key_heads = key_heads.transpose(2, 0, 1, 3).reshape(head_count, tokens_here * reflections, width)
    value_heads = reflect_values.reshape(tokens_here, reflections, head_count, width)
    value_heads = value_heads.transpose(2, 0, 1, 3).reshape(head_count, tokens_here * reflections, width)
    strengths = 2.0 * jax.nn.sigmoid(beta_logit.transpose(1, 2, 0).reshape(head_count, tokens_here * reflections))
    return (query_heads, key_heads, value_heads, strengths)

def mixer(queries, reflect_keys, reflect_values, beta_logit, start_state, head_count, block_tokens, with_transition):
    query_heads, key_heads, value_heads, strengths = arrange(queries, reflect_keys, reflect_values, beta_logit, head_count)
    width = query_heads.shape[2]
    tokens_here = query_heads.shape[1]
    reflections = key_heads.shape[1] // tokens_here
    blocks = tokens_here // block_tokens
    pseudo = block_tokens * reflections
    query_steps = query_heads.reshape(head_count, blocks, block_tokens, width).transpose(1, 0, 2, 3)
    key_steps = key_heads.reshape(head_count, blocks, pseudo, width).transpose(1, 0, 2, 3)
    value_steps = value_heads.reshape(head_count, blocks, pseudo, width).transpose(1, 0, 2, 3)
    beta_steps = strengths.reshape(head_count, blocks, pseudo).transpose(1, 0, 2)
    identity = jnp.broadcast_to(jnp.eye(width, dtype=start_state.dtype), start_state.shape)

    def advance(carry, block_items):
        carry_state, transition = carry
        query_block, key_block, value_block, beta_block = block_items
        mixed_block, next_state, key_weights = block_core(carry_state, query_block, key_block, value_block, beta_block)
        if with_transition:
            projected = jnp.einsum('hab,hnb->han', transition, key_weights, precision=HIGHEST_PRECISION)
            transition = transition - jnp.einsum('han,hnk->hak', projected, key_block, precision=HIGHEST_PRECISION)
        return ((next_state, transition), mixed_block)
    (end_state, transition), mixed_steps = lax.scan(advance, (start_state, identity), (query_steps, key_steps, value_steps, beta_steps))
    mixed_out = mixed_steps.transpose(0, 2, 1, 3).reshape(tokens_here, head_count * width)
    return ((mixed_out, end_state), transition)

def reference(queries, reflect_keys, reflect_values, beta_logit, out_weight, out_grad):
    zero_state = jnp.zeros((HEADS, HEAD_DIM, HEAD_DIM), jnp.float32)

    def forward(query_arg, key_arg, value_arg, logit_arg):
        (mixed_out, end_state), transition = mixer(query_arg, key_arg, value_arg, logit_arg, zero_state, HEADS, BLOCK, False)
        return mixed_out
    mixed_out, pull_back = jax.vjp(forward, queries, reflect_keys, reflect_values, beta_logit)
    mixed_bf = mixed_out.astype(jnp.bfloat16)
    output = jnp.dot(mixed_bf.astype(jnp.float32), out_weight.astype(jnp.float32), preferred_element_type=jnp.float32).astype(jnp.bfloat16)
    mixed_grad = jnp.dot(out_grad.astype(jnp.float32), out_weight.T.astype(jnp.float32), preferred_element_type=jnp.float32)
    query_grad, key_grad, value_grad, logit_grad = pull_back(mixed_grad)
    weight_grad = jnp.dot(mixed_bf.T.astype(jnp.float32), out_grad.astype(jnp.float32), preferred_element_type=jnp.float32)
    return (output, query_grad, key_grad, value_grad, logit_grad, weight_grad)
```

```python
import jax
import jax.numpy as jnp
from jax import lax
from jax.experimental import pallas as pl
from jax.experimental.pallas import tpu as pltpu
from jax.sharding import PartitionSpec as P

HEAD_DIM = 128
BLOCK = 64
ROWS = 2 * BLOCK
f32 = jnp.float32
bf16 = jnp.bfloat16
NN = (((1,), (0,)), ((), ()))
NT = (((1,), (1,)), ((), ()))
TN = (((0,), (0,)), ((), ()))
VMEM_LIMIT = 48 * 1024 * 1024


def halves(x):
    high = x.astype(bf16)
    return high, (x - high.astype(f32)).astype(bf16)


def dot(a, b, dims):
    return lax.dot_general(a, b, dims, preferred_element_type=f32)


def product(a, b, dims=NN):
    ah, al = a if isinstance(a, tuple) else halves(a)
    bh, bl = b if isinstance(b, tuple) else halves(b)
    return dot(ah, bh, dims) + (dot(ah, bl, dims) + dot(al, bh, dims))


def inverse_norm(x):
    return lax.rsqrt(jnp.sum(x * x, axis=-1, keepdims=True) + 1e-06)


def strengths(logits):
    return 2.0 / (1.0 + jnp.exp(-logits))


def token_grid():
    row = lax.broadcasted_iota(jnp.int32, (ROWS, ROWS), 0)
    col = lax.broadcasted_iota(jnp.int32, (ROWS, ROWS), 1)
    return row & (BLOCK - 1), col & (BLOCK - 1), row >= BLOCK, col >= BLOCK


def load_pairs(ref, block):
    rows = pl.ds(block * BLOCK, BLOCK)
    return jnp.concatenate([ref[0, rows, :], ref[1, rows, :]], axis=0)


def prepare_kernel(key_ref, value_ref, logit_ref, system_ref, solved_ref, step_ref, prefix_ref):
    blocks = key_ref.shape[1] // BLOCK
    row_token, col_token, row_second, col_second = token_grid()
    row = lax.broadcasted_iota(jnp.int32, (ROWS, ROWS), 0)
    col = lax.broadcasted_iota(jnp.int32, (ROWS, ROWS), 1)
    same_token = row_token == col_token
    pair = same_token & row_second & ~col_second
    eye = row == col
    units, keys, grams, systems = [], [], [], []
    for block in range(blocks):
        key = load_pairs(key_ref, block)
        unit = key * inverse_norm(key)
        parts = halves(unit)
        units.append(unit)
        keys.append(parts)
        grams.append(product(parts, parts, NT))
    for block in range(blocks):
        strength = jnp.broadcast_to(strengths(logit_ref[0, pl.ds(block, 1), :]), (ROWS, ROWS))
        swapped = jnp.broadcast_to(strengths(logit_ref[0, pl.ds(blocks + block, 1), :]), (ROWS, ROWS))
        systems.append(
            jnp.where(eye, strength, 0.0) - jnp.where(pair, grams[block] * (strength * swapped), 0.0)
        )
    size = 1
    while size < BLOCK:
        below = ((row_token & size) != 0) & ((row_token ^ col_token) < 2 * size) & ((col_token & size) == 0)
        now = [halves(system) for system in systems]
        middle = [
            product(jnp.where(below, grams[block], 0.0), now[block]) for block in range(blocks)
        ]
        systems = [
            systems[block] - product(now[block], middle[block]) for block in range(blocks)
        ]
        size *= 2
    prefix = None
    steps = []
    for block in range(blocks):
        value = load_pairs(value_ref, block)
        system_ref[0, block] = systems[block]
        solved = product(systems[block], jnp.concatenate([units[block], value], axis=1))
        solved_ref[0, block] = solved
        moved = product(keys[block], solved, TN)
        steps.append(
            jnp.concatenate(
                [jnp.where(eye, 1.0, 0.0) - moved[:, :HEAD_DIM], moved[:, HEAD_DIM:]], axis=1
            )
        )
        step_ref[0, block] = steps[block][:, :HEAD_DIM]
    prefix = steps[0]
    prefix_ref[0, 0] = prefix
    for block in range(1, blocks):
        moved = product(steps[block][:, :HEAD_DIM], prefix)
        prefix = jnp.concatenate(
            [moved[:, :HEAD_DIM], moved[:, HEAD_DIM:] + steps[block][:, HEAD_DIM:]], axis=1
        )
        prefix_ref[0, block] = prefix


def local_kernel(query_ref, key_ref, solved_ref, step_ref, grad_ref, weight_ref, mixed_grad_ref, reach_ref, inner_ref, drive_ref, adjoint_ref):
    blocks = query_ref.shape[0] // BLOCK
    row = lax.broadcasted_iota(jnp.int32, (BLOCK, ROWS), 0)
    col = lax.broadcasted_iota(jnp.int32, (BLOCK, ROWS), 1)
    visible = (col & (BLOCK - 1)) <= row
    mixed_grad = dot(grad_ref[...], weight_ref[...], NT)
    mixed_grad_ref[...] = mixed_grad
    drives = []
    for block in range(blocks):
        rows = pl.ds(block * BLOCK, BLOCK)
        query = query_ref[rows, :]
        query = query * inverse_norm(query)
        key = load_pairs(key_ref, block)
        key = key * inverse_norm(key)
        scores = jnp.where(visible, product(query, key, NT), 0.0)
        seen = product(scores, solved_ref[0, block])
        reach = query - seen[:, :HEAD_DIM]
        reach_ref[0, block] = reach
        inner_ref[0, block] = seen[:, HEAD_DIM:]
        drive = product(reach, mixed_grad[block * BLOCK : (block + 1) * BLOCK], TN)
        drive_ref[0, block] = drive
        drives.append(drive)
    adjoint = drives[blocks - 1]
    for block in reversed(range(blocks - 1)):
        adjoint = product(step_ref[0, block], adjoint, TN) + drives[block]
    adjoint_ref[0] = adjoint


def mix_kernel(state_ref, prefix_ref, reach_ref, inner_ref, grad_ref, states_ref, mixed_ref, weight_grad_ref):
    blocks = prefix_ref.shape[1]
    start = state_ref[0]
    parts = halves(start)
    for block in range(blocks):
        state = start
        if block:
            before = prefix_ref[0, block - 1]
            state = product(before[:, :HEAD_DIM], parts) + before[:, HEAD_DIM:]
        states_ref[0, block] = state
        mixed = product(reach_ref[0, block], state) + inner_ref[0, block]
        mixed_ref[pl.ds(block * BLOCK, BLOCK), :] = mixed.astype(bf16)
    weight_grad_ref[...] = dot(mixed_ref[...], grad_ref[...], TN).astype(bf16)


def unit_pull(x, unit_grad):
    scale = inverse_norm(x)
    unit = x * scale
    return scale * (unit_grad - unit * jnp.sum(unit * unit_grad, axis=-1, keepdims=True))


def gradient_kernel(
    query_ref, key_ref, logit_ref, system_ref, solved_ref, step_ref, states_ref, drive_ref, mixed_grad_ref, adjoint_ref,
    query_grad_ref, key_grad_ref, value_grad_ref, logit_grad_ref,
):
    blocks = query_ref.shape[0] // BLOCK
    row = lax.broadcasted_iota(jnp.int32, (BLOCK, ROWS), 0)
    col = lax.broadcasted_iota(jnp.int32, (BLOCK, ROWS), 1)
    visible = (col & (BLOCK - 1)) <= row
    row_token, col_token, row_second, col_second = token_grid()
    earlier = (col_token < row_token) | ((col_token == row_token) & row_second & ~col_second)
    ones = jnp.ones((8, HEAD_DIM), bf16)
    adjoint = adjoint_ref[0]
    for block in reversed(range(blocks)):
        rows = pl.ds(block * BLOCK, BLOCK)
        query = query_ref[rows, :]
        key = load_pairs(key_ref, block)
        query_unit = halves(query * inverse_norm(query))
        key_unit = halves(key * inverse_norm(key))
        state = halves(states_ref[0, block])
        solved = solved_ref[0, block]
        fresh = solved[:, HEAD_DIM:] - product(solved[:, :HEAD_DIM], state)
        fresh_parts = halves(fresh)
        out_grad = halves(mixed_grad_ref[rows, :])
        after = halves(adjoint)
        scores = jnp.where(visible, product(query_unit, key_unit, NT), 0.0)
        fresh_grad = product(scores, out_grad, TN) + product(key_unit, after)
        value_grad = product(system_ref[0, block], fresh_grad, TN)
        value_parts = halves(value_grad)
        value_grad_ref[0, rows, :] = value_grad[:BLOCK]
        value_grad_ref[1, rows, :] = value_grad[BLOCK:]
        high, low = halves(value_grad * fresh)
        sums = dot(ones, high, NT) + dot(ones, low, NT)
        logit_grad_ref[0, pl.ds(block, 1), :] = (
            0.5 * jnp.exp(-logit_ref[0, pl.ds(block, 1), :]) * sums[0:1]
        )
        score_grad = halves(jnp.where(visible, product(out_grad, fresh_parts, NT), 0.0))
        query_unit_grad = product(out_grad, state, NT) + product(score_grad, key_unit)
        query_grad_ref[rows, :] = unit_pull(query, query_unit_grad)
        gram_grad = halves(jnp.where(earlier, product(value_parts, fresh_parts, NT), 0.0))
        key_unit_grad = (
            product(score_grad, query_unit, TN)
            + product(fresh_parts, after, NT)
            - product(value_parts, state, NT)
            - (product(gram_grad, key_unit) + product(gram_grad, key_unit, TN))
        )
        key_grad = unit_pull(key, key_unit_grad)
        key_grad_ref[0, rows, :] = key_grad[:BLOCK]
        key_grad_ref[1, rows, :] = key_grad[BLOCK:]
        if block:
            adjoint = product(step_ref[0, block], after, TN) + drive_ref[0, block]


def head_call(kernel, name, heads, outs, *operands):
    def spec(kind, shape):
        rank = len(shape)
        if kind == "first":
            return pl.BlockSpec((1, *shape[1:]), lambda h: (h,) + (0,) * (rank - 1))
        if kind == "last":
            return pl.BlockSpec((*shape[:-1], HEAD_DIM), lambda h: (0,) * (rank - 1) + (h,))
        if kind == "rows":
            return pl.BlockSpec((HEAD_DIM, *shape[1:]), lambda h: (h,) + (0,) * (rank - 1))
        return pl.BlockSpec(shape, lambda h: (0,) * rank)

    return pl.pallas_call(
        kernel,
        name=name,
        grid=(heads,),
        in_specs=[spec(kind, array.shape) for kind, array in operands],
        out_specs=[spec(kind, shape) for kind, shape, _ in outs],
        out_shape=[jax.ShapeDtypeStruct(shape, dtype) for _, shape, dtype in outs],
        compiler_params=pltpu.CompilerParams(
            dimension_semantics=("arbitrary",), vmem_limit_bytes=VMEM_LIMIT
        ),
    )(*[array for _, array in operands])


def shifted(array, by):
    count = lax.axis_size("seq")
    pairs = [(i, i + by) for i in range(count) if 0 <= i + by < count]
    return lax.ppermute(array, "seq", pairs)


def joined(later, earlier):
    moved = jnp.einsum(
        "hab,hbn->han", later[:, :, :HEAD_DIM], earlier, precision=lax.Precision.HIGHEST
    )
    return moved + jnp.concatenate([jnp.zeros_like(moved[:, :, :HEAD_DIM]), later[:, :, HEAD_DIM:]], axis=2)


def arriving(own, sign):
    count = lax.axis_size("seq")
    distance = 1
    while distance < count // 2:
        own = joined(own, shifted(own, sign * distance))
        distance *= 2
    near = shifted(own, sign)
    if count == 1:
        return near[:, :, HEAD_DIM:]
    far = shifted(own[:, :, HEAD_DIM:], sign * (count // 2 + 1))
    return near[:, :, HEAD_DIM:] + jnp.einsum(
        "hab,hbn->han", near[:, :, :HEAD_DIM], far, precision=lax.Precision.HIGHEST
    )


def gathered(array, axis):
    copies = jnp.broadcast_to(array[None], (lax.axis_size(axis), *array.shape))
    return lax.all_to_all(copies, axis, 0, 0, tiled=True)


def project_kernel(mixed_ref, weight_ref, out_ref):
    total = dot(mixed_ref[0], weight_ref[0], NN)
    for part in range(1, mixed_ref.shape[0]):
        total = total + dot(mixed_ref[part], weight_ref[part], NN)
    out_ref[...] = total.astype(bf16)


def body(queries, reflect_keys, reflect_values, beta_logit, out_weight, out_grad):
    tokens, features = queries.shape
    heads = features // HEAD_DIM
    blocks = tokens // BLOCK
    square = (heads, blocks, ROWS, HEAD_DIM)
    double = (heads, blocks, ROWS, 2 * HEAD_DIM)
    keys = reflect_keys.transpose(1, 0, 2)
    values = reflect_values.transpose(1, 0, 2)
    logits = beta_logit.reshape(2, heads, blocks, BLOCK).transpose(1, 2, 0, 3)
    logit_rows = jnp.concatenate(
        [logits.reshape(heads, blocks, ROWS), logits[:, :, ::-1].reshape(heads, blocks, ROWS)], axis=1
    )
    parts = lax.axis_size("head")
    grad_parts = gathered(out_grad, "head")
    weight_parts = lax.all_to_all(
        out_weight.reshape(features, parts, features).transpose(1, 0, 2), "head", 0, 0, tiled=True
    )
    full_grad = grad_parts.transpose(1, 0, 2).reshape(tokens, parts * features)

    system, solved, step, prefix = head_call(
        prepare_kernel,
        "prepare",
        heads,
        [("first", square, f32), ("first", double, f32), ("first", square, f32), ("first", double, f32)],
        ("last", keys),
        ("last", values),
        ("first", logit_rows),
    )
    whole = prefix[:, -1]
    state_in = arriving(whole, 1)
    mixed_grad, reach, inner, drive, adjoint = head_call(
        local_kernel,
        "local",
        heads,
        [
            ("last", (tokens, features), f32),
            ("first", (heads, blocks, BLOCK, HEAD_DIM), f32),
            ("first", (heads, blocks, BLOCK, HEAD_DIM), f32),
            ("first", square, f32),
            ("first", (heads, ROWS, HEAD_DIM), f32),
        ],
        ("last", queries),
        ("last", keys),
        ("first", solved),
        ("first", step),
        ("whole", full_grad),
        ("rows", out_weight),
    )
    adjoint_in = arriving(
        jnp.concatenate([jnp.swapaxes(whole[:, :, :HEAD_DIM], 1, 2), adjoint], axis=2), -1
    )
    states, mixed, weight_share = head_call(
        mix_kernel,
        "mix",
        heads,
        [("first", square, f32), ("last", (tokens, features), bf16), ("rows", out_weight.shape, bf16)],
        ("first", state_in),
        ("first", prefix),
        ("first", reach),
        ("first", inner),
        ("whole", full_grad),
    )
    seq_count = lax.axis_size("seq")
    weight_grad = jnp.sum(
        lax.all_to_all(
            weight_share.reshape(seq_count, features // seq_count, out_weight.shape[1]), "seq", 0, 0, tiled=True
        ).astype(f32),
        axis=0,
    )
    output = pl.pallas_call(
        project_kernel,
        name="project",
        out_shape=jax.ShapeDtypeStruct((tokens, features), bf16),
        compiler_params=pltpu.CompilerParams(vmem_limit_bytes=VMEM_LIMIT),
    )(gathered(mixed, "head"), weight_parts)
    query_grad, key_grad, value_grad, logit_grad = head_call(
        gradient_kernel,
        "gradients",
        heads,
        [
            ("last", queries.shape, f32),
            ("last", keys.shape, f32),
            ("last", values.shape, f32),
            ("first", (heads, blocks, ROWS), f32),
        ],
        ("last", queries),
        ("last", keys),
        ("first", logit_rows),
        ("first", system),
        ("first", solved),
        ("first", step),
        ("first", states),
        ("first", drive),
        ("last", mixed_grad),
        ("first", adjoint_in),
    )
    logit_grad = logit_grad.reshape(heads, blocks, 2, BLOCK).transpose(2, 0, 1, 3).reshape(beta_logit.shape)
    return (
        output,
        query_grad,
        key_grad.transpose(1, 0, 2),
        value_grad.transpose(1, 0, 2),
        logit_grad,
        weight_grad,
    )


def solution(mesh):
    in_specs = (
        P("seq", "head"),
        P("seq", None, "head"),
        P("seq", None, "head"),
        P(None, "head", "seq"),
        P("head", None),
        P("seq", "head"),
    )
    out_specs = (
        P("seq", "head"),
        P("seq", "head"),
        P("seq", None, "head"),
        P("seq", None, "head"),
        P(None, "head", "seq"),
        P(("head", "seq"), None),
    )
    return jax.shard_map(body, mesh=mesh, in_specs=in_specs, out_specs=out_specs, check_vma=False)
```

```python
import functools

import jax
import jax.numpy as jnp
from jax import lax
from jax.experimental import pallas as pl
from jax.experimental.pallas import tpu as pltpu
from jax.sharding import PartitionSpec as P

HEAD_DIM = 128
BLOCK = 64
ROWS = 2 * BLOCK
RING = 8
f32 = jnp.float32
bf16 = jnp.bfloat16
NN = (((1,), (0,)), ((), ()))
NT = (((1,), (1,)), ((), ()))
TN = (((0,), (0,)), ((), ()))
VMEM_LIMIT = 24 * 1024 * 1024


def halves(x):
    high = x.astype(bf16)
    return high, (x - high.astype(f32)).astype(bf16)


def dot(a, b, dims):
    return lax.dot_general(a, b, dims, preferred_element_type=f32)


def product(a, b, dims=NN):
    ah, al = a if isinstance(a, tuple) else halves(a)
    bh, bl = b if isinstance(b, tuple) else halves(b)
    return dot(ah, bh, dims) + (dot(ah, bl, dims) + dot(al, bh, dims))


def inverse_norm(x):
    return lax.rsqrt(jnp.sum(x * x, axis=-1, keepdims=True) + 1e-06)


def strengths(logits):
    return 2.0 / (1.0 + jnp.exp(-logits))


def token_grid():
    row = lax.broadcasted_iota(jnp.int32, (ROWS, ROWS), 0)
    col = lax.broadcasted_iota(jnp.int32, (ROWS, ROWS), 1)
    return row & (BLOCK - 1), col & (BLOCK - 1), row >= BLOCK, col >= BLOCK


def load_pairs(ref, block):
    rows = pl.ds(block * BLOCK, BLOCK)
    return jnp.concatenate([ref[rows, 0, :], ref[rows, 1, :]], axis=0)


def prepare_kernel(
    key_ref, value_ref, logit_ref, system_ref, solved_ref, step_ref, prefix_ref, whole_ref
):
    blocks = key_ref.shape[0] // BLOCK
    row_token, col_token, row_second, col_second = token_grid()
    row = lax.broadcasted_iota(jnp.int32, (ROWS, ROWS), 0)
    col = lax.broadcasted_iota(jnp.int32, (ROWS, ROWS), 1)
    same_token = row_token == col_token
    pair = same_token & row_second & ~col_second
    eye = row == col
    units, keys, grams, systems = [], [], [], []
    for block in range(blocks):
        key = load_pairs(key_ref, block)
        unit = key * inverse_norm(key)
        parts = halves(unit)
        units.append(unit)
        keys.append(parts)
        grams.append(product(parts, parts, NT))
    for block in range(blocks):
        strength = jnp.broadcast_to(strengths(logit_ref[0, pl.ds(block, 1), :]), (ROWS, ROWS))
        swapped = jnp.broadcast_to(strengths(logit_ref[0, pl.ds(blocks + block, 1), :]), (ROWS, ROWS))
        systems.append(
            jnp.where(eye, strength, 0.0) - jnp.where(pair, grams[block] * (strength * swapped), 0.0)
        )
    size = 1
    while size < BLOCK:
        below = ((row_token & size) != 0) & ((row_token ^ col_token) < 2 * size) & ((col_token & size) == 0)
        now = [halves(system) for system in systems]
        middle = [
            product(jnp.where(below, grams[block], 0.0), now[block]) for block in range(blocks)
        ]
        systems = [
            systems[block] - product(now[block], middle[block]) for block in range(blocks)
        ]
        size *= 2
    prefix = None
    steps = []
    for block in range(blocks):
        value = load_pairs(value_ref, block)
        system_ref[0, block] = systems[block]
        solved = product(systems[block], jnp.concatenate([units[block], value], axis=1))
        solved_ref[0, block] = solved
        moved = product(keys[block], solved, TN)
        steps.append(
            jnp.concatenate(
                [jnp.where(eye, 1.0, 0.0) - moved[:, :HEAD_DIM], moved[:, HEAD_DIM:]], axis=1
            )
        )
        step_ref[0, block] = steps[block][:, :HEAD_DIM]
    prefix = steps[0]
    prefix_ref[0, 0] = prefix
    for block in range(1, blocks):
        moved = product(steps[block][:, :HEAD_DIM], prefix)
        prefix = jnp.concatenate(
            [moved[:, :HEAD_DIM], moved[:, HEAD_DIM:] + steps[block][:, HEAD_DIM:]], axis=1
        )
        prefix_ref[0, block] = prefix
    whole_ref[0] = prefix


def columns(place_ref, mask, width):
    return pl.ds(pl.multiple_of((place_ref[0] ^ mask) * width, width), width)


def local_kernel(place_ref, query_ref, key_ref, solved_ref, step_ref, weight_ref, *refs):
    grad_refs = refs[:-5]
    mixed_grad_ref, reach_ref, inner_ref, drive_ref, adjoint_ref = refs[-5:]
    blocks = query_ref.shape[0] // BLOCK
    row = lax.broadcasted_iota(jnp.int32, (BLOCK, ROWS), 0)
    col = lax.broadcasted_iota(jnp.int32, (BLOCK, ROWS), 1)
    visible = (col & (BLOCK - 1)) <= row
    mixed_grad = None
    for mask, grad_ref in enumerate(grad_refs):
        term = dot(grad_ref[...], weight_ref[:, columns(place_ref, mask, grad_ref.shape[1])], NT)
        mixed_grad = term if mixed_grad is None else mixed_grad + term
    mixed_grad_ref[...] = mixed_grad
    drives = []
    for block in range(blocks):
        rows = pl.ds(block * BLOCK, BLOCK)
        query = query_ref[rows, :]
        query = query * inverse_norm(query)
        key = load_pairs(key_ref, block)
        key = key * inverse_norm(key)
        scores = jnp.where(visible, product(query, key, NT), 0.0)
        seen = product(scores, solved_ref[0, block])
        reach = query - seen[:, :HEAD_DIM]
        reach_ref[0, block] = reach
        inner_ref[0, block] = seen[:, HEAD_DIM:]
        drive = product(reach, mixed_grad[block * BLOCK : (block + 1) * BLOCK], TN)
        drive_ref[0, block] = drive
        drives.append(drive)
    adjoint = drives[blocks - 1]
    for block in reversed(range(blocks - 1)):
        adjoint = product(step_ref[0, block], adjoint, TN) + drives[block]
    adjoint_ref[0] = adjoint


def merge_kernel(first, upper_ref, next_upper_ref, own_ref, far_ref, *refs):
    extra_refs, refs = refs[:2], refs[2:]
    before_out, after_out, send_ref = refs[:3]
    total_out = refs[3] if len(refs) > 3 else None
    upper = upper_ref[0] == 1
    d = HEAD_DIM
    for head in range(own_ref.shape[0]):
        own = own_ref[head]
        far = far_ref[head].astype(f32)
        if first:
            own = jnp.concatenate([own, extra_refs[0][head]], axis=1)
            far = jnp.concatenate([far, extra_refs[1][head]], axis=1)
        low = jnp.where(upper, far, own)
        high = jnp.where(upper, own, far)
        low_parts, high_parts = halves(low), halves(high)
        head_of = lambda parts, cut: tuple(part[:, cut] for part in parts)
        forward = product(head_of(high_parts, slice(0, d)), head_of(low_parts, slice(0, 2 * d)))
        state = forward[:, d:] + high[:, d : 2 * d]
        adjoint = product(head_of(low_parts, slice(0, d)), head_of(high_parts, slice(2 * d, 3 * d)), TN) + low[:, 2 * d :]
        step = forward[:, :d]
        far_step = far[:, :d]
        beside = jnp.where(
            upper, far[:, : 2 * d], jnp.concatenate([far_step.T, far[:, 2 * d :]], axis=1)
        )
        if first:
            identity = jnp.where(
                lax.broadcasted_iota(jnp.int32, (d, 2 * d), 0) == lax.broadcasted_iota(jnp.int32, (d, 2 * d), 1), 1.0, 0.0
            )
            before_out[head] = jnp.where(upper, beside, identity)
            after_out[head] = jnp.where(upper, identity, beside)
        else:
            before, after = extra_refs[0][head], extra_refs[1][head]
            near = jnp.where(upper, before, after)
            moved = product(near[:, :d], beside)
            moved = jnp.concatenate([moved[:, :d], moved[:, d:] + near[:, d:]], axis=1)
            before_out[head] = jnp.where(upper, moved, before)
            after_out[head] = jnp.where(upper, after, moved)
        if total_out is None:
            send_ref[head] = jnp.where(next_upper_ref[0] == 1, adjoint, state).astype(send_ref.dtype)
        else:
            total = jnp.concatenate([step, state, adjoint], axis=1)
            total_out[head] = total
            send_ref[head] = total.astype(send_ref.dtype)


def mix_kernel(
    place_ref, upper_ref, before_ref, after_ref, far_ref, prefix_ref, reach_ref, inner_ref, *refs
):
    grad_refs = refs[:-4]
    states_ref, adjoint_ref, mixed_ref, weight_grad_ref = refs[-4:]
    blocks = prefix_ref.shape[1]
    upper = upper_ref[0] == 1
    before, after = before_ref[0], after_ref[0]
    near = jnp.where(upper, before, after)
    moved = product(near[:, :HEAD_DIM], far_ref[0].astype(f32)) + near[:, HEAD_DIM:]
    start = jnp.where(upper, moved, before[:, HEAD_DIM:])
    adjoint_ref[0] = jnp.where(upper, after[:, HEAD_DIM:], moved)
    parts = halves(start)
    for block in range(blocks):
        state = start
        if block:
            ahead = prefix_ref[0, block - 1]
            state = product(ahead[:, :HEAD_DIM], parts) + ahead[:, HEAD_DIM:]
        states_ref[0, block] = state
        mixed = product(reach_ref[0, block], state) + inner_ref[0, block]
        mixed_ref[pl.ds(block * BLOCK, BLOCK), :] = mixed.astype(bf16)
    mixed = mixed_ref[...]
    for mask, grad_ref in enumerate(grad_refs):
        part = columns(place_ref, mask, grad_ref.shape[1])
        weight_grad_ref[:, part] = dot(mixed, grad_ref[...], TN).astype(bf16)


def unit_pull(x, unit_grad):
    scale = inverse_norm(x)
    unit = x * scale
    return scale * (unit_grad - unit * jnp.sum(unit * unit_grad, axis=-1, keepdims=True))


def gradient_kernel(
    query_ref, key_ref, logit_ref, system_ref, solved_ref, step_ref, states_ref, drive_ref, mixed_grad_ref, adjoint_ref,
    query_grad_ref, key_grad_ref, value_grad_ref, logit_grad_ref,
):
    blocks = query_ref.shape[0] // BLOCK
    row = lax.broadcasted_iota(jnp.int32, (BLOCK, ROWS), 0)
    col = lax.broadcasted_iota(jnp.int32, (BLOCK, ROWS), 1)
    visible = (col & (BLOCK - 1)) <= row
    row_token, col_token, row_second, col_second = token_grid()
    earlier = (col_token < row_token) | ((col_token == row_token) & row_second & ~col_second)
    ones = jnp.ones((8, HEAD_DIM), bf16)
    adjoint = adjoint_ref[0]
    for block in reversed(range(blocks)):
        rows = pl.ds(block * BLOCK, BLOCK)
        query = query_ref[rows, :]
        key = load_pairs(key_ref, block)
        query_unit = halves(query * inverse_norm(query))
        key_unit = halves(key * inverse_norm(key))
        state = halves(states_ref[0, block])
        solved = solved_ref[0, block]
        fresh = solved[:, HEAD_DIM:] - product(solved[:, :HEAD_DIM], state)
        fresh_parts = halves(fresh)
        out_grad = halves(mixed_grad_ref[rows, :])
        after = halves(adjoint)
        scores = jnp.where(visible, product(query_unit, key_unit, NT), 0.0)
        fresh_grad = product(scores, out_grad, TN) + product(key_unit, after)
        value_grad = product(system_ref[0, block], fresh_grad, TN)
        value_parts = halves(value_grad)
        value_grad_ref[rows, 0, :] = value_grad[:BLOCK]
        value_grad_ref[rows, 1, :] = value_grad[BLOCK:]
        high, low = halves(value_grad * fresh)
        sums = dot(ones, high, NT) + dot(ones, low, NT)
        logit_grad_ref[0, pl.ds(block, 1), :] = (
            0.5 * jnp.exp(-logit_ref[0, pl.ds(block, 1), :]) * sums[0:1]
        )
        score_grad = halves(jnp.where(visible, product(out_grad, fresh_parts, NT), 0.0))
        query_unit_grad = product(out_grad, state, NT) + product(score_grad, key_unit)
        query_grad_ref[rows, :] = unit_pull(query, query_unit_grad)
        gram_grad = halves(jnp.where(earlier, product(value_parts, fresh_parts, NT), 0.0))
        key_unit_grad = (
            product(score_grad, query_unit, TN)
            + product(fresh_parts, after, NT)
            - product(value_parts, state, NT)
            - (product(gram_grad, key_unit) + product(gram_grad, key_unit, TN))
        )
        key_grad = unit_pull(key, key_unit_grad)
        key_grad_ref[rows, 0, :] = key_grad[:BLOCK]
        key_grad_ref[rows, 1, :] = key_grad[BLOCK:]
        if block:
            adjoint = product(step_ref[0, block], after, TN) + drive_ref[0, block]


def head_call(kernel, name, heads, outs, *operands):
    def spec(kind, shape):
        rank = len(shape)
        if kind in ("first", "free"):
            return pl.BlockSpec((1, *shape[1:]), lambda h: (h,) + (0,) * (rank - 1))
        if kind == "last":
            return pl.BlockSpec((*shape[:-1], HEAD_DIM), lambda h: (0,) * (rank - 1) + (h,))
        if kind == "scalar":
            return pl.BlockSpec(memory_space=pltpu.SMEM)
        if kind == "rows":
            return pl.BlockSpec((HEAD_DIM, *shape[1:]), lambda h: (h,) + (0,) * (rank - 1))
        return pl.BlockSpec(shape, lambda h: (0,) * rank)

    return pl.pallas_call(
        kernel,
        name=name,
        grid=(heads,),
        in_specs=[spec(kind, array.shape) for kind, array in operands],
        out_specs=[spec(kind, shape) for kind, shape, _ in outs],
        out_shape=[pltpu.HBM(shape, dtype) for _, shape, dtype in outs],
        compiler_params=pltpu.CompilerParams(
            dimension_semantics=("arbitrary",), vmem_limit_bytes=VMEM_LIMIT
        ),
    )(
        *[
            array if kind in ("scalar", "free", "whole free") else pltpu.with_memory_space_constraint(array, pltpu.HBM)
            for kind, array in operands
        ]
    )


def exchanged(array, axis, mask):
    return lax.ppermute(array, axis, [(i, i ^ mask) for i in range(lax.axis_size(axis))])


def merged(first, upper, next_upper, own, far, extra, send_dtype, last):
    heads = own.shape[0]
    near = ("first", (heads, HEAD_DIM, 2 * HEAD_DIM), f32)
    outs = [near, near]
    if last:
        outs += [("first", (heads, HEAD_DIM, HEAD_DIM), send_dtype)]
    else:
        whole = (heads, HEAD_DIM, 3 * HEAD_DIM)
        outs += [("first", whole, send_dtype), ("first", whole, f32)]
    return head_call(
        functools.partial(merge_kernel, first),
        "merge",
        heads,
        outs,
        ("scalar", upper),
        ("scalar", next_upper),
        ("first", own),
        ("free", far),
        ("first", extra[0]),
        ("free" if first else "first", extra[1]),
    )


def level_masks(count):
    masks, size = [], 1
    while size < count:
        masks.append(2 * size - 1 if size < RING else 2 * size - RING)
        size *= 2
    return masks


def gathered(array, axis):
    return [array] + [exchanged(array, axis, mask) for mask in range(1, lax.axis_size(axis))]


def project_kernel(place_ref, weight_ref, *refs):
    out_ref = refs[-1]
    total = None
    for mask, mixed_ref in enumerate(refs[:-1]):
        term = dot(mixed_ref[...], weight_ref[place_ref[0] ^ mask], NN)
        total = term if total is None else total + term
    out_ref[...] = total.astype(bf16)


def body(queries, reflect_keys, reflect_values, beta_logit, out_weight, out_grad):
    tokens, features = queries.shape
    heads = features // HEAD_DIM
    blocks = tokens // BLOCK
    square = (heads, blocks, ROWS, HEAD_DIM)
    double = (heads, blocks, ROWS, 2 * HEAD_DIM)
    parts = lax.axis_size("head")
    seq_count = lax.axis_size("seq")
    place = lax.axis_index("seq")
    head_place = lax.axis_index("head").astype(jnp.int32).reshape(1)
    grad_parts = gathered(out_grad, "head")
    keys, values = reflect_keys, reflect_values
    logits = beta_logit.reshape(2, heads, blocks, BLOCK).transpose(1, 2, 0, 3)
    logit_rows = jnp.concatenate(
        [logits.reshape(heads, blocks, ROWS), logits[:, :, ::-1].reshape(heads, blocks, ROWS)], axis=1
    )

    system, solved, step, prefix, whole = head_call(
        prepare_kernel,
        "prepare",
        heads,
        [
            ("first", square, f32),
            ("first", double, f32),
            ("first", square, f32),
            ("first", double, f32),
            ("first", (heads, HEAD_DIM, 2 * HEAD_DIM), f32),
        ],
        ("last", keys),
        ("last", values),
        ("first", logit_rows),
    )
    masks = level_masks(seq_count)
    far = exchanged(whole, "seq", masks[0])
    weight_source, whole = lax.optimization_barrier((out_weight, whole))
    weight_parts = lax.all_to_all(
        weight_source.reshape(features, parts, features).transpose(1, 0, 2), "head", 0, 0, tiled=True
    )
    mixed_grad, reach, inner, drive, adjoint = head_call(
        local_kernel,
        "local",
        heads,
        [
            ("last", (tokens, features), f32),
            ("first", (heads, blocks, BLOCK, HEAD_DIM), f32),
            ("first", (heads, blocks, BLOCK, HEAD_DIM), f32),
            ("first", square, f32),
            ("first", (heads, ROWS, HEAD_DIM), f32),
        ],
        ("scalar", head_place),
        ("last", queries),
        ("last", keys),
        ("first", solved),
        ("first", step),
        ("rows", out_weight),
        *[("whole free", part) for part in grad_parts],
    )
    far_tail = exchanged(adjoint, "seq", masks[0])
    total, extra = whole, (adjoint, far_tail)
    upper = [((place >> level) & 1).astype(jnp.int32).reshape(1) for level in range(len(masks))]
    for level in range(len(masks) - 1):
        last = level == len(masks) - 2
        send_dtype = bf16 if 0 <= level < 2 and not last else f32
        result = merged(
            level == 0, upper[level], upper[level + 1], total, far, extra, send_dtype, last
        )
        extra, sent = result[:2], result[2]
        total = None if last else result[3]
        far = exchanged(sent, "seq", masks[level + 1])
    states, adjoint_in, mixed, weight_share = head_call(
        mix_kernel,
        "mix",
        heads,
        [
            ("first", square, f32),
            ("first", (heads, ROWS, HEAD_DIM), f32),
            ("last", (tokens, features), bf16),
            ("rows", out_weight.shape, bf16),
        ],
        ("scalar", head_place),
        ("scalar", upper[-1]),
        ("first", extra[0]),
        ("first", extra[1]),
        ("free", far),
        ("first", prefix),
        ("first", reach),
        ("first", inner),
        *[("whole", part) for part in grad_parts],
    )
    weight_grad = jnp.sum(
        lax.all_to_all(
            weight_share.reshape(seq_count, features // seq_count, out_weight.shape[1]), "seq", 0, 0, tiled=True
        ).astype(f32),
        axis=0,
    )
    query_grad, key_grad, value_grad, logit_grad = head_call(
        gradient_kernel,
        "gradients",
        heads,
        [
            ("last", queries.shape, f32),
            ("last", keys.shape, f32),
            ("last", values.shape, f32),
            ("first", (heads, blocks, ROWS), f32),
        ],
        ("last", queries),
        ("last", keys),
        ("first", logit_rows),
        ("first", system),
        ("first", solved),
        ("first", step),
        ("first", states),
        ("first", drive),
        ("last", mixed_grad),
        ("first", adjoint_in),
    )
    mixed_parts = gathered(mixed, "head")
    vmem = pl.BlockSpec(memory_space=pltpu.VMEM)
    output = pl.pallas_call(
        project_kernel,
        name="project",
        in_specs=[pl.BlockSpec(memory_space=pltpu.SMEM)] + [vmem] * (1 + parts),
        out_specs=vmem,
        out_shape=jax.ShapeDtypeStruct((tokens, features), bf16),
        compiler_params=pltpu.CompilerParams(vmem_limit_bytes=VMEM_LIMIT),
    )(head_place, weight_parts, *mixed_parts)
    logit_grad = logit_grad.reshape(heads, blocks, 2, BLOCK).transpose(2, 0, 1, 3).reshape(beta_logit.shape)
    return (
        output,
        query_grad,
        key_grad,
        value_grad,
        logit_grad,
        weight_grad,
    )


def solution(mesh):
    in_specs = (
        P("seq", "head"),
        P("seq", None, "head"),
        P("seq", None, "head"),
        P(None, "head", "seq"),
        P("head", None),
        P("seq", "head"),
    )
    out_specs = (
        P("seq", "head"),
        P("seq", "head"),
        P("seq", None, "head"),
        P("seq", None, "head"),
        P(None, "head", "seq"),
        P(("head", "seq"), None),
    )
    return jax.shard_map(body, mesh=mesh, in_specs=in_specs, out_specs=out_specs, check_vma=False)
```

```python
import functools

import jax
import jax.numpy as jnp
from jax import lax
from jax.experimental import pallas as pl
from jax.experimental.pallas import tpu as pltpu
from jax.sharding import PartitionSpec as P

HEAD_DIM = 128
BLOCK = 64
ROWS = 2 * BLOCK
RING = 8
f32 = jnp.float32
bf16 = jnp.bfloat16
NN = (((1,), (0,)), ((), ()))
NT = (((1,), (1,)), ((), ()))
TN = (((0,), (0,)), ((), ()))
SCALE = 1_000_000_000
COST = {
    "prepare": 9, "local": 5, "merge": 2, "merge_adjoint": 2, "cut": 2, "mix": 5, "gradients": 10, "project": 2
}
VMEM_LIMIT = 24 * 1024 * 1024


def halves(x):
    high = x.astype(bf16)
    return high, (x - high.astype(f32)).astype(bf16)


def dot(a, b, dims):
    return lax.dot_general(a, b, dims, preferred_element_type=f32)


def product(a, b, dims=NN):
    ah, al = a if isinstance(a, tuple) else halves(a)
    bh, bl = b if isinstance(b, tuple) else halves(b)
    (a_axis,), (b_axis,) = dims[0]
    wide = jnp.concatenate([bh, bl], axis=1 - b_axis)
    both = dot(jnp.concatenate([ah, al], axis=a_axis), jnp.concatenate([wide, wide], axis=b_axis), dims)
    cut = both.shape[1] // 2
    return both[:, :cut] + both[:, cut:]


def inverse_norm(x):
    return lax.rsqrt(jnp.sum(x * x, axis=-1, keepdims=True) + 1e-06)


def strengths(logits):
    return 2.0 / (1.0 + jnp.exp(-logits))


def token_grid():
    row = lax.broadcasted_iota(jnp.int32, (ROWS, ROWS), 0)
    col = lax.broadcasted_iota(jnp.int32, (ROWS, ROWS), 1)
    return row & (BLOCK - 1), col & (BLOCK - 1), row >= BLOCK, col >= BLOCK


def load_pairs(ref, block):
    rows = pl.ds(block * BLOCK, BLOCK)
    return jnp.concatenate([ref[rows, 0, :], ref[rows, 1, :]], axis=0)


def prepare_kernel(
    query_ref, key_ref, value_ref, logit_ref,
    system_ref, solved_ref, step_ref, prefix_ref, whole_ref, reach_ref, inner_ref,
):
    blocks = key_ref.shape[0] // BLOCK
    row_token, col_token, row_second, col_second = token_grid()
    row = lax.broadcasted_iota(jnp.int32, (ROWS, ROWS), 0)
    col = lax.broadcasted_iota(jnp.int32, (ROWS, ROWS), 1)
    same_token = row_token == col_token
    pair = same_token & row_second & ~col_second
    eye = row == col
    visible = col_token[:BLOCK] <= row_token[:BLOCK]
    units, keys, grams, systems = [], [], [], []
    for block in range(blocks):
        key = load_pairs(key_ref, block)
        unit = key * inverse_norm(key)
        parts = halves(unit)
        units.append(unit)
        keys.append(parts)
        grams.append(product(parts, parts, NT))
    for block in range(blocks):
        strength = jnp.broadcast_to(strengths(logit_ref[0, pl.ds(block, 1), :]), (ROWS, ROWS))
        swapped = jnp.broadcast_to(strengths(logit_ref[0, pl.ds(blocks + block, 1), :]), (ROWS, ROWS))
        systems.append(
            jnp.where(eye, strength, 0.0) - jnp.where(pair, grams[block] * (strength * swapped), 0.0)
        )
    size = 1
    while size < BLOCK:
        below = ((row_token & size) != 0) & ((row_token ^ col_token) < 2 * size) & ((col_token & size) == 0)
        now = [halves(system) for system in systems]
        middle = [
            product(jnp.where(below, grams[block], 0.0), now[block]) for block in range(blocks)
        ]
        systems = [
            systems[block] - product(now[block], middle[block]) for block in range(blocks)
        ]
        size *= 2
    prefix = None
    steps = []
    for block in range(blocks):
        value = load_pairs(value_ref, block)
        system_ref[0, block] = systems[block]
        solved = product(systems[block], jnp.concatenate([units[block], value], axis=1))
        solved_ref[0, block] = solved
        solved_parts = halves(solved)
        moved = product(keys[block], solved_parts, TN)
        steps.append(
            jnp.concatenate(
                [jnp.where(eye, 1.0, 0.0) - moved[:, :HEAD_DIM], moved[:, HEAD_DIM:]], axis=1
            )
        )
        step_ref[0, block] = steps[block][:, :HEAD_DIM]
        query = query_ref[pl.ds(block * BLOCK, BLOCK), :]
        query = query * inverse_norm(query)
        scores = jnp.where(visible, product(query, keys[block], NT), 0.0)
        seen = product(scores, solved_parts)
        reach_ref[0, block] = query - seen[:, :HEAD_DIM]
        inner_ref[0, block] = seen[:, HEAD_DIM:]
    prefix = steps[0]
    prefix_ref[0, 0] = prefix
    for block in range(1, blocks):
        moved = product(steps[block][:, :HEAD_DIM], prefix)
        prefix = jnp.concatenate(
            [moved[:, :HEAD_DIM], moved[:, HEAD_DIM:] + steps[block][:, HEAD_DIM:]], axis=1
        )
        prefix_ref[0, block] = prefix
    whole_ref[0] = prefix


def columns(place_ref, mask, width):
    return pl.ds(pl.multiple_of((place_ref[0] ^ mask) * width, width), width)


def local_kernel(place_ref, reach_ref, step_ref, weight_ref, *refs):
    grad_refs = refs[:-3]
    mixed_grad_ref, drive_ref, adjoint_ref = refs[-3:]
    blocks = reach_ref.shape[1]
    mixed_grad = None
    for mask, grad in each(grad_refs):
        term = dot(grad, weight_ref[:, columns(place_ref, mask, grad.shape[1])], NT)
        mixed_grad = term if mixed_grad is None else mixed_grad + term
    mixed_grad_ref[...] = mixed_grad
    drives = []
    for block in range(blocks):
        drive = product(reach_ref[0, block], mixed_grad[block * BLOCK : (block + 1) * BLOCK], TN)
        drive_ref[0, block] = drive
        drives.append(drive)
    adjoint = drives[blocks - 1]
    for block in reversed(range(blocks - 1)):
        adjoint = product(step_ref[0, block], adjoint, TN) + drives[block]
    adjoint_ref[0] = adjoint


def identity(width):
    row = lax.broadcasted_iota(jnp.int32, (HEAD_DIM, width), 0)
    return jnp.where(row == lax.broadcasted_iota(jnp.int32, (HEAD_DIM, width), 1), 1.0, 0.0)


def merge_kernel(first, last, upper_ref, own_ref, far_ref, *refs):
    before_ref, after_ref = (None, None) if first else refs[:2]
    before_out, after_out, low_out, send_ref = refs[-4:] if last else refs[-5:-1]
    upper = upper_ref[0] == 1
    d = HEAD_DIM
    for head in range(own_ref.shape[0]):
        own, far = own_ref[head], far_ref[head].astype(f32)
        low, high = jnp.where(upper, far, own), jnp.where(upper, own, far)
        cut = d if last else 0
        total = product(high[:, :d], low[:, cut:])
        total = total + high[:, d:] if last else jnp.concatenate([total[:, :d], total[:, d:] + high[:, d:]], axis=1)
        send_ref[head] = total.astype(send_ref.dtype)
        low_out[head] = low[:, :d]
        if not last:
            refs[-1][head] = total
        back = far[:, :d].T
        if first:
            before_out[head] = jnp.where(upper, far, identity(2 * d))
            after_out[head] = jnp.where(upper, identity(d), back)
        else:
            before, after = before_ref[head], after_ref[head]
            beside = jnp.where(upper, far, jnp.concatenate([back, jnp.zeros_like(back)], axis=1))
            moved = product(jnp.where(upper, before[:, :d], after), beside)
            ahead = jnp.concatenate([moved[:, :d], moved[:, d:] + before[:, d:]], axis=1)
            before_out[head] = jnp.where(upper, ahead, before)
            after_out[head] = jnp.where(upper, after, moved[:, :d])


def adjoint_kernel(first, upper_ref, own_ref, far_ref, low_ref, *refs):
    after_ref, behind_ref = (None, None) if first else refs[:2]
    behind_out, send_ref, total_out = refs[-3:]
    upper = upper_ref[0] == 1
    for head in range(own_ref.shape[0]):
        own, far = own_ref[head], far_ref[head].astype(f32)
        low, high = jnp.where(upper, far, own), jnp.where(upper, own, far)
        total = product(low_ref[head], high, TN) + low
        total_out[head] = total
        send_ref[head] = total.astype(send_ref.dtype)
        if first:
            behind_out[head] = jnp.where(upper, 0.0, far)
        else:
            behind = behind_ref[head]
            behind_out[head] = jnp.where(upper, behind, product(after_ref[head], far) + behind)


def mix_kernel(place_ref, before_ref, far_ref, prefix_ref, reach_ref, inner_ref, *refs):
    grad_refs = refs[:-3]
    states_ref, mixed_ref, weight_grad_ref = refs[-3:]
    blocks = prefix_ref.shape[1]
    before = before_ref[0]
    start = product(before[:, :HEAD_DIM], far_ref[0]) + before[:, HEAD_DIM:]
    parts = halves(start)
    for block in range(blocks):
        state = start
        if block:
            ahead = prefix_ref[0, block - 1]
            state = product(ahead[:, :HEAD_DIM], parts) + ahead[:, HEAD_DIM:]
        states_ref[0, block] = state
        mixed = product(reach_ref[0, block], state) + inner_ref[0, block]
        mixed_ref[pl.ds(block * BLOCK, BLOCK), :] = mixed.astype(bf16)
    mixed = mixed_ref[...]
    for mask, grad in each(grad_refs):
        part = columns(place_ref, mask, grad.shape[1])
        weight_grad_ref[:, part] = dot(mixed, grad, TN).astype(bf16)


def unit_pull(x, unit_grad):
    scale = inverse_norm(x)
    unit = x * scale
    return scale * (unit_grad - unit * jnp.sum(unit * unit_grad, axis=-1, keepdims=True))


def gradient_kernel(
    query_ref, key_ref, logit_ref, system_ref, solved_ref, step_ref, states_ref, drive_ref, mixed_grad_ref,
    after_ref, behind_ref, far_ref,
    query_grad_ref, key_grad_ref, value_grad_ref, logit_grad_ref,
):
    blocks = query_ref.shape[0] // BLOCK
    row = lax.broadcasted_iota(jnp.int32, (BLOCK, ROWS), 0)
    col = lax.broadcasted_iota(jnp.int32, (BLOCK, ROWS), 1)
    visible = (col & (BLOCK - 1)) <= row
    row_token, col_token, row_second, col_second = token_grid()
    earlier = (col_token < row_token) | ((col_token == row_token) & row_second & ~col_second)
    ones = jnp.ones((8, HEAD_DIM), bf16)
    adjoint = product(after_ref[0], far_ref[0]) + behind_ref[0]
    for block in reversed(range(blocks)):
        rows = pl.ds(block * BLOCK, BLOCK)
        query = query_ref[rows, :]
        key = load_pairs(key_ref, block)
        query_unit = halves(query * inverse_norm(query))
        key_unit = halves(key * inverse_norm(key))
        state = halves(states_ref[0, block])
        solved = solved_ref[0, block]
        fresh = solved[:, HEAD_DIM:] - product(solved[:, :HEAD_DIM], state)
        fresh_parts = halves(fresh)
        out_grad = halves(mixed_grad_ref[rows, :])
        after = halves(adjoint)
        scores = jnp.where(visible, product(query_unit, key_unit, NT), 0.0)
        fresh_grad = product(scores, out_grad, TN) + product(key_unit, after)
        value_grad = product(system_ref[0, block], fresh_grad, TN)
        value_parts = halves(value_grad)
        value_grad_ref[rows, 0, :] = value_grad[:BLOCK]
        value_grad_ref[rows, 1, :] = value_grad[BLOCK:]
        high, low = halves(value_grad * fresh)
        sums = dot(ones, high, NT) + dot(ones, low, NT)
        logit_grad_ref[0, pl.ds(block, 1), :] = (
            0.5 * jnp.exp(-logit_ref[0, pl.ds(block, 1), :]) * sums[0:1]
        )
        score_grad = halves(jnp.where(visible, product(out_grad, fresh_parts, NT), 0.0))
        query_unit_grad = product(out_grad, state, NT) + product(score_grad, key_unit)
        query_grad_ref[rows, :] = unit_pull(query, query_unit_grad)
        gram_grad = halves(jnp.where(earlier, product(value_parts, fresh_parts, NT), 0.0))
        key_unit_grad = (
            product(score_grad, query_unit, TN)
            + product(fresh_parts, after, NT)
            - product(value_parts, state, NT)
            - (product(gram_grad, key_unit) + product(gram_grad, key_unit, TN))
        )
        key_grad = unit_pull(key, key_unit_grad)
        key_grad_ref[rows, 0, :] = key_grad[:BLOCK]
        key_grad_ref[rows, 1, :] = key_grad[BLOCK:]
        if block:
            adjoint = product(step_ref[0, block], after, TN) + drive_ref[0, block]


def head_call(kernel, name, heads, outs, *operands, steps=None, following=()):
    def spec(kind, shape):
        rank = len(shape)
        if steps == 1 and kind != "scalar":
            return pl.BlockSpec(shape, lambda h: (0,) * rank)
        if kind in ("first", "free"):
            return pl.BlockSpec((1, *shape[1:]), lambda h: (h,) + (0,) * (rank - 1))
        if kind == "last":
            return pl.BlockSpec((*shape[:-1], HEAD_DIM), lambda h: (0,) * (rank - 1) + (h,))
        if kind == "scalar":
            return pl.BlockSpec(memory_space=pltpu.SMEM)
        if kind == "rows":
            return pl.BlockSpec((HEAD_DIM, *shape[1:]), lambda h: (h,) + (0,) * (rank - 1))
        return pl.BlockSpec(shape, lambda h: (0,) * rank)

    def run(*refs):
        kernel(*refs[len(following) :])

    return pl.pallas_call(
        run,
        name=name,
        grid=(steps or heads,),
        in_specs=[pl.BlockSpec(memory_space=pl.ANY)] * len(following)
        + [spec(kind, array.shape) for kind, array in operands],
        out_specs=[spec(kind, shape) for kind, shape, _ in outs],
        out_shape=[pltpu.HBM(shape, dtype) for _, shape, dtype in outs],
        cost_estimate=pl.CostEstimate(flops=COST[name] * SCALE, bytes_accessed=0, transcendentals=0),
        compiler_params=pltpu.CompilerParams(
            dimension_semantics=("arbitrary",), vmem_limit_bytes=VMEM_LIMIT
        ),
    )(
        *[pltpu.with_memory_space_constraint(array, pltpu.HBM) for array in following],
        *[
            array if kind in ("scalar", "free", "whole free") else pltpu.with_memory_space_constraint(array, pltpu.HBM)
            for kind, array in operands
        ]
    )


def exchanged(array, axis, mask):
    return lax.ppermute(array, axis, [(i, i ^ mask) for i in range(lax.axis_size(axis))])


def passed(array, mask, to_upper):
    half = (mask + 1) // 2 if mask < RING else mask & ~(mask >> 1)
    pairs = [(i, i ^ mask) for i in range(lax.axis_size("seq")) if ((i & half) == 0) == to_upper]
    return lax.ppermute(array, "seq", pairs)


def level_masks(count):
    masks, size = [], 1
    while size < count:
        masks.append(2 * size - 1 if size < RING else 2 * size - RING)
        size *= 2
    return masks


def gathered(array, axis):
    if lax.axis_size(axis) == 1:
        return [array[None]]
    pair = jnp.stack([array, exchanged(array, axis, 1)])
    return [pair] + [exchanged(pair, axis, mask) for mask in range(2, lax.axis_size(axis), 2)]


def each(refs):
    for place, ref in enumerate(refs):
        for part in range(ref.shape[0]):
            yield 2 * place + part, ref[part]


def cut_kernel(weight_ref, out_ref):
    width = out_ref.shape[2]
    for part in range(out_ref.shape[0]):
        out_ref[part] = weight_ref[:, part * width : (part + 1) * width]


def project_kernel(place_ref, weight_ref, *refs):
    out_ref = refs[-1]
    total = None
    for mask, mixed in each(refs[:-1]):
        term = dot(mixed, weight_ref[place_ref[0] ^ mask], NN)
        total = term if total is None else total + term
    out_ref[...] = total.astype(bf16)


def body(queries, reflect_keys, reflect_values, beta_logit, out_weight, out_grad):
    tokens, features = queries.shape
    heads = features // HEAD_DIM
    blocks = tokens // BLOCK
    square = (heads, blocks, ROWS, HEAD_DIM)
    double = (heads, blocks, ROWS, 2 * HEAD_DIM)
    parts = lax.axis_size("head")
    seq_count = lax.axis_size("seq")
    place = lax.axis_index("seq")
    head_place = lax.axis_index("head").astype(jnp.int32).reshape(1)
    grad_parts = gathered(out_grad, "head")
    keys, values = reflect_keys, reflect_values
    logits = beta_logit.reshape(2, heads, blocks, BLOCK).transpose(1, 2, 0, 3)
    logit_rows = jnp.concatenate(
        [logits.reshape(heads, blocks, ROWS), logits[:, :, ::-1].reshape(heads, blocks, ROWS)], axis=1
    )

    system, solved, step, prefix, whole, reach, inner = head_call(
        prepare_kernel,
        "prepare",
        heads,
        [
            ("first", square, f32),
            ("first", double, f32),
            ("first", square, f32),
            ("first", double, f32),
            ("first", (heads, HEAD_DIM, 2 * HEAD_DIM), f32),
            ("first", (heads, blocks, BLOCK, HEAD_DIM), f32),
            ("first", (heads, blocks, BLOCK, HEAD_DIM), f32),
        ],
        ("last", queries),
        ("last", keys),
        ("last", values),
        ("first", logit_rows),
    )
    masks = level_masks(seq_count)
    far = exchanged(whole, "seq", masks[0])
    mixed_grad, drive, adjoint = head_call(
        local_kernel,
        "local",
        heads,
        [
            ("last", (tokens, features), f32),
            ("first", square, f32),
            ("first", (heads, ROWS, HEAD_DIM), f32),
        ],
        ("scalar", head_place),
        ("first", reach),
        ("first", step),
        ("rows", out_weight),
        *[("whole free", part) for part in grad_parts],
    )
    upper = [((place >> level) & 1).astype(jnp.int32).reshape(1) for level in range(len(masks))]
    tile = (heads, HEAD_DIM, HEAD_DIM)
    wide = (heads, HEAD_DIM, 2 * HEAD_DIM)
    far_adjoint = exchanged(adjoint, "seq", masks[0])
    levels = len(masks) - 1
    total, before, after, behind = whole, None, None, None
    held = []

    def join_adjoint(level, following):
        nonlocal behind, adjoint, far_adjoint
        first, last = level == 0, level == levels - 1
        low, after_before = held[level]
        send_dtype = bf16 if level < 2 and not last else f32
        behind, sent, adjoint = head_call(
            functools.partial(adjoint_kernel, first),
            "merge_adjoint",
            heads,
            [("first", tile, f32), ("first", tile, send_dtype), ("first", tile, f32)],
            ("scalar", upper[level]),
            ("first", adjoint),
            ("free", far_adjoint),
            ("first", low),
            *([] if first else [("first", after_before), ("first", behind)]),
            steps=1,
            following=following,
        )
        far_adjoint = (
            passed(sent, masks[-1], False) if last else exchanged(sent, "seq", masks[level + 1])
        )

    for level in range(levels):
        first, last = level == 0, level == levels - 1
        if level >= 1:
            join_adjoint(level - 1, ())
        if level == min(2, levels - 1):
            (weight_cut,) = head_call(
                cut_kernel,
                "cut",
                heads,
                [("whole", (parts, features, features), bf16)],
                ("whole", out_weight),
                steps=1,
                following=(adjoint,),
            )
            weight_parts = lax.all_to_all(weight_cut, "head", 0, 0, tiled=True)
        send_dtype = bf16 if level < 2 and not last else f32
        before_join = after
        before, after, low, sent, *rest = head_call(
            functools.partial(merge_kernel, first, last),
            "merge",
            heads,
            [("first", wide, f32), ("first", tile, f32), ("first", tile, f32)]
            + ([("first", tile, f32)] if last else [("first", wide, send_dtype), ("first", wide, f32)]),
            ("scalar", upper[level]),
            ("first", total),
            ("free", far),
            *([] if first else [("first", before), ("first", after)]),
            steps=1,
            following=(adjoint, weight_cut) if level == 3 else (adjoint,),
        )
        held.append((low, before_join))
        total = rest[0] if rest else None
        far = passed(sent, masks[-1], True) if last else exchanged(sent, "seq", masks[level + 1])
    join_adjoint(levels - 1, ())
    states, mixed, weight_share = head_call(
        mix_kernel,
        "mix",
        heads,
        [("first", square, f32), ("last", (tokens, features), bf16), ("rows", out_weight.shape, bf16)],
        ("scalar", head_place),
        ("first", before),
        ("free", far),
        ("first", prefix),
        ("first", reach),
        ("first", inner),
        *[("whole", part) for part in grad_parts],
        following=(adjoint,),
    )
    weight_grad = jnp.sum(
        lax.all_to_all(
            weight_share.reshape(seq_count, features // seq_count, out_weight.shape[1]), "seq", 0, 0, tiled=True
        ).astype(f32),
        axis=0,
    )
    query_grad, key_grad, value_grad, logit_grad = head_call(
        gradient_kernel,
        "gradients",
        heads,
        [
            ("last", queries.shape, f32),
            ("last", keys.shape, f32),
            ("last", values.shape, f32),
            ("first", (heads, blocks, ROWS), f32),
        ],
        ("last", queries),
        ("last", keys),
        ("first", logit_rows),
        ("first", system),
        ("first", solved),
        ("first", step),
        ("first", states),
        ("first", drive),
        ("last", mixed_grad),
        ("first", after),
        ("first", behind),
        ("free", far_adjoint),
    )
    mixed_parts = gathered(mixed, "head")
    vmem = pl.BlockSpec(memory_space=pltpu.VMEM)
    output = pl.pallas_call(
        project_kernel,
        name="project",
        in_specs=[pl.BlockSpec(memory_space=pltpu.SMEM)] + [vmem] * (1 + len(mixed_parts)),
        out_specs=vmem,
        out_shape=jax.ShapeDtypeStruct((tokens, features), bf16),
        compiler_params=pltpu.CompilerParams(vmem_limit_bytes=VMEM_LIMIT),
    )(head_place, weight_parts, *mixed_parts)
    logit_grad = logit_grad.reshape(heads, blocks, 2, BLOCK).transpose(2, 0, 1, 3).reshape(beta_logit.shape)
    return (
        output,
        query_grad,
        key_grad,
        value_grad,
        logit_grad,
        weight_grad,
    )


def solution(mesh):
    in_specs = (
        P("seq", "head"),
        P("seq", None, "head"),
        P("seq", None, "head"),
        P(None, "head", "seq"),
        P("head", None),
        P("seq", "head"),
    )
    out_specs = (
        P("seq", "head"),
        P("seq", "head"),
        P("seq", None, "head"),
        P("seq", None, "head"),
        P(None, "head", "seq"),
        P(("head", "seq"), None),
    )
    return jax.shard_map(body, mesh=mesh, in_specs=in_specs, out_specs=out_specs, check_vma=False)
```

```python
import functools

import jax
import jax.numpy as jnp
from jax import lax
from jax.experimental import pallas as pl
from jax.experimental.pallas import tpu as pltpu
from jax.sharding import PartitionSpec as P

HEAD_DIM = 128
BLOCK = 64
ROWS = 2 * BLOCK
RING = 8
f32 = jnp.float32
bf16 = jnp.bfloat16
NN = (((1,), (0,)), ((), ()))
NT = (((1,), (1,)), ((), ()))
TN = (((0,), (0,)), ((), ()))
SCALE = 2_000_000_000
COST = {
    "prepare": 9, "local": 5, "merge": 2, "merge_adjoint": 2, "mix": 5, "gradients": 3, "project": 3
}
VMEM_LIMIT = 24 * 1024 * 1024


def halves(x):
    high = x.astype(bf16)
    return high, (x - high.astype(f32)).astype(bf16)


def dot(a, b, dims):
    return lax.dot_general(a, b, dims, preferred_element_type=f32)


def product(a, b, dims=NN):
    ah, al = a if isinstance(a, tuple) else halves(a)
    bh, bl = b if isinstance(b, tuple) else halves(b)
    (a_axis,), (b_axis,) = dims[0]
    wide = jnp.concatenate([bh, bl], axis=1 - b_axis)
    both = dot(jnp.concatenate([ah, al], axis=a_axis), jnp.concatenate([wide, wide], axis=b_axis), dims)
    cut = both.shape[1] // 2
    return both[:, :cut] + both[:, cut:]


def inverse_norm(x):
    return lax.rsqrt(jnp.sum(x * x, axis=-1, keepdims=True) + 1e-06)


def strengths(logits):
    return 2.0 / (1.0 + jnp.exp(-logits))


def token_grid():
    row = lax.broadcasted_iota(jnp.int32, (ROWS, ROWS), 0)
    col = lax.broadcasted_iota(jnp.int32, (ROWS, ROWS), 1)
    return row & (BLOCK - 1), col & (BLOCK - 1), row >= BLOCK, col >= BLOCK


def load_pairs(ref, block):
    rows = pl.ds(block * BLOCK, BLOCK)
    return jnp.concatenate([ref[rows, 0, :], ref[rows, 1, :]], axis=0)


def prepare_kernel(
    query_ref, key_ref, value_ref, logit_ref,
    system_ref, solved_ref, step_ref, prefix_ref, whole_ref, reach_ref, inner_ref,
):
    blocks = key_ref.shape[0] // BLOCK
    row_token, col_token, row_second, col_second = token_grid()
    row = lax.broadcasted_iota(jnp.int32, (ROWS, ROWS), 0)
    col = lax.broadcasted_iota(jnp.int32, (ROWS, ROWS), 1)
    same_token = row_token == col_token
    pair = same_token & row_second & ~col_second
    eye = row == col
    visible = col_token[:BLOCK] <= row_token[:BLOCK]
    units, keys, grams, systems = [], [], [], []
    for block in range(blocks):
        key = load_pairs(key_ref, block)
        unit = key * inverse_norm(key)
        parts = halves(unit)
        units.append(unit)
        keys.append(parts)
        grams.append(product(parts, parts, NT))
    for block in range(blocks):
        strength = jnp.broadcast_to(strengths(logit_ref[0, pl.ds(block, 1), :]), (ROWS, ROWS))
        swapped = jnp.broadcast_to(strengths(logit_ref[0, pl.ds(blocks + block, 1), :]), (ROWS, ROWS))
        systems.append(
            jnp.where(eye, strength, 0.0) - jnp.where(pair, grams[block] * (strength * swapped), 0.0)
        )
    size = 1
    while size < BLOCK:
        below = ((row_token & size) != 0) & ((row_token ^ col_token) < 2 * size) & ((col_token & size) == 0)
        now = [halves(system) for system in systems]
        middle = [
            product(jnp.where(below, grams[block], 0.0), now[block]) for block in range(blocks)
        ]
        systems = [
            systems[block] - product(now[block], middle[block]) for block in range(blocks)
        ]
        size *= 2
    prefix = None
    steps = []
    for block in range(blocks):
        value = load_pairs(value_ref, block)
        system_ref[0, block] = systems[block]
        solved = product(systems[block], jnp.concatenate([units[block], value], axis=1))
        solved_ref[0, block] = solved
        solved_parts = halves(solved)
        moved = product(keys[block], solved_parts, TN)
        steps.append(
            jnp.concatenate(
                [jnp.where(eye, 1.0, 0.0) - moved[:, :HEAD_DIM], moved[:, HEAD_DIM:]], axis=1
            )
        )
        step_ref[0, block] = steps[block][:, :HEAD_DIM]
        query = query_ref[pl.ds(block * BLOCK, BLOCK), :]
        query = query * inverse_norm(query)
        scores = jnp.where(visible, product(query, keys[block], NT), 0.0)
        seen = product(scores, solved_parts)
        reach_ref[0, block] = query - seen[:, :HEAD_DIM]
        inner_ref[0, block] = seen[:, HEAD_DIM:]
    prefix = steps[0]
    prefix_ref[0, 0] = prefix
    for block in range(1, blocks):
        moved = product(steps[block][:, :HEAD_DIM], prefix)
        prefix = jnp.concatenate(
            [moved[:, :HEAD_DIM], moved[:, HEAD_DIM:] + steps[block][:, HEAD_DIM:]], axis=1
        )
        prefix_ref[0, block] = prefix
    whole_ref[0] = prefix


def columns(place_ref, mask, width):
    return pl.ds(pl.multiple_of((place_ref[0] ^ mask) * width, width), width)


def local_kernel(place_ref, reach_ref, step_ref, weight_ref, *refs):
    grad_refs = refs[:-3]
    mixed_grad_ref, drive_ref, adjoint_ref = refs[-3:]
    blocks = reach_ref.shape[1]
    mixed_grad = None
    for mask, grad in each(grad_refs):
        term = dot(grad, weight_ref[:, columns(place_ref, mask, grad.shape[1])], NT)
        mixed_grad = term if mixed_grad is None else mixed_grad + term
    mixed_grad_ref[...] = mixed_grad
    drives = []
    for block in range(blocks):
        drive = product(reach_ref[0, block], mixed_grad[block * BLOCK : (block + 1) * BLOCK], TN)
        drive_ref[0, block] = drive
        drives.append(drive)
    adjoint = drives[blocks - 1]
    for block in reversed(range(blocks - 1)):
        adjoint = product(step_ref[0, block], adjoint, TN) + drives[block]
    adjoint_ref[0] = adjoint


def identity(width):
    row = lax.broadcasted_iota(jnp.int32, (HEAD_DIM, width), 0)
    return jnp.where(row == lax.broadcasted_iota(jnp.int32, (HEAD_DIM, width), 1), 1.0, 0.0)


def merge_kernel(first, last, upper_ref, own_ref, far_ref, *refs):
    before_ref, after_ref = (None, None) if first else refs[:2]
    before_out, after_out, low_out, send_ref = refs[-4:] if last else refs[-5:-1]
    upper = upper_ref[0] == 1
    d = HEAD_DIM
    for head in range(own_ref.shape[0]):
        own, far = own_ref[head], far_ref[head].astype(f32)
        low, high = jnp.where(upper, far, own), jnp.where(upper, own, far)
        cut = d if last else 0
        total = product(high[:, :d], low[:, cut:])
        total = total + high[:, d:] if last else jnp.concatenate([total[:, :d], total[:, d:] + high[:, d:]], axis=1)
        send_ref[head] = total.astype(send_ref.dtype)
        low_out[head] = low[:, :d]
        if not last:
            refs[-1][head] = total
        back = far[:, :d].T
        if first:
            before_out[head] = jnp.where(upper, far, identity(2 * d))
            after_out[head] = jnp.where(upper, identity(d), back)
        else:
            before, after = before_ref[head], after_ref[head]
            beside = jnp.where(upper, far, jnp.concatenate([back, jnp.zeros_like(back)], axis=1))
            moved = product(jnp.where(upper, before[:, :d], after), beside)
            ahead = jnp.concatenate([moved[:, :d], moved[:, d:] + before[:, d:]], axis=1)
            before_out[head] = jnp.where(upper, ahead, before)
            after_out[head] = jnp.where(upper, after, moved[:, :d])


def adjoint_kernel(first, upper_ref, own_ref, far_ref, low_ref, *refs):
    after_ref, behind_ref = (None, None) if first else refs[:2]
    behind_out, send_ref, total_out = refs[-3:]
    upper = upper_ref[0] == 1
    for head in range(own_ref.shape[0]):
        own, far = own_ref[head], far_ref[head].astype(f32)
        low, high = jnp.where(upper, far, own), jnp.where(upper, own, far)
        total = product(low_ref[head], high, TN) + low
        total_out[head] = total
        send_ref[head] = total.astype(send_ref.dtype)
        if first:
            behind_out[head] = jnp.where(upper, 0.0, far)
        else:
            behind = behind_ref[head]
            behind_out[head] = jnp.where(upper, behind, product(after_ref[head], far) + behind)


def mix_kernel(place_ref, before_ref, far_ref, prefix_ref, reach_ref, inner_ref, *refs):
    grad_refs = refs[:-3]
    states_ref, mixed_ref, weight_grad_ref = refs[-3:]
    blocks = prefix_ref.shape[1]
    before = before_ref[0]
    start = product(before[:, :HEAD_DIM], far_ref[0]) + before[:, HEAD_DIM:]
    parts = halves(start)
    for block in range(blocks):
        state = start
        if block:
            ahead = prefix_ref[0, block - 1]
            state = product(ahead[:, :HEAD_DIM], parts) + ahead[:, HEAD_DIM:]
        states_ref[0, block] = state
        mixed = product(reach_ref[0, block], state) + inner_ref[0, block]
        mixed_ref[pl.ds(block * BLOCK, BLOCK), :] = mixed.astype(bf16)
    mixed = mixed_ref[...]
    for mask, grad in each(grad_refs):
        part = columns(place_ref, mask, grad.shape[1])
        weight_grad_ref[:, part] = dot(mixed, grad, TN).astype(bf16)


def unit_pull(x, unit_grad):
    scale = inverse_norm(x)
    unit = x * scale
    return scale * (unit_grad - unit * jnp.sum(unit * unit_grad, axis=-1, keepdims=True))


def gradient_kernel(
    query_ref, key_ref, logit_ref, system_ref, solved_ref, step_ref, states_ref, drive_ref, mixed_grad_ref,
    after_ref, behind_ref, far_ref,
    query_grad_ref, key_grad_ref, value_grad_ref, logit_grad_ref,
):
    blocks = query_ref.shape[0] // BLOCK
    row = lax.broadcasted_iota(jnp.int32, (BLOCK, ROWS), 0)
    col = lax.broadcasted_iota(jnp.int32, (BLOCK, ROWS), 1)
    visible = (col & (BLOCK - 1)) <= row
    row_token, col_token, row_second, col_second = token_grid()
    earlier = (col_token < row_token) | ((col_token == row_token) & row_second & ~col_second)
    ones = jnp.ones((8, HEAD_DIM), bf16)
    adjoint = product(after_ref[0], far_ref[0]) + behind_ref[0]
    for block in reversed(range(blocks)):
        rows = pl.ds(block * BLOCK, BLOCK)
        query = query_ref[rows, :]
        key = load_pairs(key_ref, block)
        query_unit = halves(query * inverse_norm(query))
        key_unit = halves(key * inverse_norm(key))
        state = halves(states_ref[0, block])
        solved = solved_ref[0, block]
        fresh = solved[:, HEAD_DIM:] - product(solved[:, :HEAD_DIM], state)
        fresh_parts = halves(fresh)
        out_grad = halves(mixed_grad_ref[rows, :])
        after = halves(adjoint)
        scores = jnp.where(visible, product(query_unit, key_unit, NT), 0.0)
        fresh_grad = product(scores, out_grad, TN) + product(key_unit, after)
        value_grad = product(system_ref[0, block], fresh_grad, TN)
        value_parts = halves(value_grad)
        value_grad_ref[rows, 0, :] = value_grad[:BLOCK]
        value_grad_ref[rows, 1, :] = value_grad[BLOCK:]
        high, low = halves(value_grad * fresh)
        sums = dot(ones, high, NT) + dot(ones, low, NT)
        logit_grad_ref[0, pl.ds(block, 1), :] = (
            0.5 * jnp.exp(-logit_ref[0, pl.ds(block, 1), :]) * sums[0:1]
        )
        score_grad = halves(jnp.where(visible, product(out_grad, fresh_parts, NT), 0.0))
        query_unit_grad = product(out_grad, state, NT) + product(score_grad, key_unit)
        query_grad_ref[rows, :] = unit_pull(query, query_unit_grad)
        gram_grad = halves(jnp.where(earlier, product(value_parts, fresh_parts, NT), 0.0))
        key_unit_grad = (
            product(score_grad, query_unit, TN)
            + product(fresh_parts, after, NT)
            - product(value_parts, state, NT)
            - (product(gram_grad, key_unit) + product(gram_grad, key_unit, TN))
        )
        key_grad = unit_pull(key, key_unit_grad)
        key_grad_ref[rows, 0, :] = key_grad[:BLOCK]
        key_grad_ref[rows, 1, :] = key_grad[BLOCK:]
        if block:
            adjoint = product(step_ref[0, block], after, TN) + drive_ref[0, block]


def head_call(kernel, name, heads, outs, *operands, steps=None, following=()):
    def spec(kind, shape):
        rank = len(shape)
        if steps == 1 and kind != "scalar":
            return pl.BlockSpec(shape, lambda h: (0,) * rank)
        if kind in ("first", "free"):
            return pl.BlockSpec((1, *shape[1:]), lambda h: (h,) + (0,) * (rank - 1))
        if kind == "last":
            return pl.BlockSpec((*shape[:-1], HEAD_DIM), lambda h: (0,) * (rank - 1) + (h,))
        if kind == "scalar":
            return pl.BlockSpec(memory_space=pltpu.SMEM)
        if kind == "rows":
            return pl.BlockSpec((HEAD_DIM, *shape[1:]), lambda h: (h,) + (0,) * (rank - 1))
        return pl.BlockSpec(shape, lambda h: (0,) * rank)

    def run(*refs):
        kernel(*refs[len(following) :])

    return pl.pallas_call(
        run,
        name=name,
        grid=(steps or heads,),
        in_specs=[pl.BlockSpec(memory_space=pl.ANY)] * len(following)
        + [spec(kind, array.shape) for kind, array in operands],
        out_specs=[spec(kind, shape) for kind, shape, _ in outs],
        out_shape=[
            jax.ShapeDtypeStruct(shape, dtype) if kind == "free" else pltpu.HBM(shape, dtype)
            for kind, shape, dtype in outs
        ],
        cost_estimate=pl.CostEstimate(flops=COST[name] * SCALE, bytes_accessed=0, transcendentals=0),
        compiler_params=pltpu.CompilerParams(
            dimension_semantics=("arbitrary",), vmem_limit_bytes=VMEM_LIMIT
        ),
    )(
        *[pltpu.with_memory_space_constraint(array, pltpu.HBM) for array in following],
        *[
            array if kind in ("scalar", "free", "whole free") else pltpu.with_memory_space_constraint(array, pltpu.HBM)
            for kind, array in operands
        ]
    )


def exchanged(array, axis, mask):
    return lax.ppermute(array, axis, [(i, i ^ mask) for i in range(lax.axis_size(axis))])


def passed(array, mask, to_upper):
    half = (mask + 1) // 2 if mask < RING else mask & ~(mask >> 1)
    pairs = [(i, i ^ mask) for i in range(lax.axis_size("seq")) if ((i & half) == 0) == to_upper]
    return lax.ppermute(array, "seq", pairs)


def level_masks(count):
    masks, size = [], 1
    while size < count:
        masks.append(2 * size - 1 if size < RING else 2 * size - RING)
        size *= 2
    return masks


def gathered(array, axis):
    if lax.axis_size(axis) == 1:
        return [array[None]]
    pair = jnp.stack([array, exchanged(array, axis, 1)])
    return [pair] + [exchanged(pair, axis, mask) for mask in range(2, lax.axis_size(axis), 2)]


def each(refs):
    for place, ref in enumerate(refs):
        for part in range(ref.shape[0]):
            yield 2 * place + part, ref[part]


def project_kernel(place_ref, mixed_ref, weight_ref, own_ref, *sent_refs):
    mixed = mixed_ref[...]
    for mask, ref in enumerate((own_ref, *sent_refs)):
        share = dot(mixed, weight_ref[:, columns(place_ref, mask, ref.shape[1])], NN)
        ref[...] = share.astype(ref.dtype)


def body(queries, reflect_keys, reflect_values, beta_logit, out_weight, out_grad):
    tokens, features = queries.shape
    heads = features // HEAD_DIM
    blocks = tokens // BLOCK
    square = (heads, blocks, ROWS, HEAD_DIM)
    double = (heads, blocks, ROWS, 2 * HEAD_DIM)
    parts = lax.axis_size("head")
    seq_count = lax.axis_size("seq")
    place = lax.axis_index("seq")
    head_place = lax.axis_index("head").astype(jnp.int32).reshape(1)
    grad_parts = gathered(out_grad, "head")
    keys, values = reflect_keys, reflect_values
    logits = beta_logit.reshape(2, heads, blocks, BLOCK).transpose(1, 2, 0, 3)
    logit_rows = jnp.concatenate(
        [logits.reshape(heads, blocks, ROWS), logits[:, :, ::-1].reshape(heads, blocks, ROWS)], axis=1
    )

    system, solved, step, prefix, whole, reach, inner = head_call(
        prepare_kernel,
        "prepare",
        heads,
        [
            ("first", square, f32),
            ("first", double, f32),
            ("first", square, f32),
            ("first", double, f32),
            ("first", (heads, HEAD_DIM, 2 * HEAD_DIM), f32),
            ("first", (heads, blocks, BLOCK, HEAD_DIM), f32),
            ("first", (heads, blocks, BLOCK, HEAD_DIM), f32),
        ],
        ("last", queries),
        ("last", keys),
        ("last", values),
        ("first", logit_rows),
    )
    masks = level_masks(seq_count)
    far = exchanged(whole, "seq", masks[0])
    mixed_grad, drive, adjoint = head_call(
        local_kernel,
        "local",
        heads,
        [
            ("last", (tokens, features), f32),
            ("first", square, f32),
            ("first", (heads, ROWS, HEAD_DIM), f32),
        ],
        ("scalar", head_place),
        ("first", reach),
        ("first", step),
        ("rows", out_weight),
        *[("whole free", part) for part in grad_parts],
    )
    upper = [((place >> level) & 1).astype(jnp.int32).reshape(1) for level in range(len(masks))]
    tile = (heads, HEAD_DIM, HEAD_DIM)
    wide = (heads, HEAD_DIM, 2 * HEAD_DIM)
    far_adjoint = exchanged(adjoint, "seq", masks[0])
    levels = len(masks) - 1
    total, before, after, behind = whole, None, None, None
    held = []

    def join_adjoint(level, following):
        nonlocal behind, adjoint, far_adjoint
        first, last = level == 0, level == levels - 1
        low, after_before = held[level]
        send_dtype = bf16 if level < 2 and not last else f32
        behind, sent, adjoint = head_call(
            functools.partial(adjoint_kernel, first),
            "merge_adjoint",
            heads,
            [("first", tile, f32), ("free", tile, send_dtype), ("first", tile, f32)],
            ("scalar", upper[level]),
            ("first", adjoint),
            ("free", far_adjoint),
            ("first", low),
            *([] if first else [("first", after_before), ("first", behind)]),
            steps=1,
            following=following,
        )
        far_adjoint = (
            passed(sent, masks[-1], False) if last else exchanged(sent, "seq", masks[level + 1])
        )

    for level in range(levels):
        first, last = level == 0, level == levels - 1
        if level >= 1:
            join_adjoint(level - 1, ())
        send_dtype = bf16 if level < 2 and not last else f32
        before_join = after
        before, after, low, sent, *rest = head_call(
            functools.partial(merge_kernel, first, last),
            "merge",
            heads,
            [("first", wide, f32), ("first", tile, f32), ("first", tile, f32)]
            + ([("first", tile, f32)] if last else [("first", wide, send_dtype), ("first", wide, f32)]),
            ("scalar", upper[level]),
            ("first", total),
            ("free", far),
            *([] if first else [("first", before), ("first", after)]),
            steps=1,
            following=(adjoint,),
        )
        held.append((low, before_join))
        total = rest[0] if rest else None
        far = passed(sent, masks[-1], True) if last else exchanged(sent, "seq", masks[level + 1])
    join_adjoint(levels - 1, ())
    states, mixed, weight_share = head_call(
        mix_kernel,
        "mix",
        heads,
        [("first", square, f32), ("last", (tokens, features), bf16), ("rows", out_weight.shape, bf16)],
        ("scalar", head_place),
        ("first", before),
        ("free", far),
        ("first", prefix),
        ("first", reach),
        ("first", inner),
        *[("whole", part) for part in grad_parts],
        following=(adjoint,),
    )
    weight_grad = jnp.sum(
        lax.all_to_all(
            weight_share.reshape(seq_count, features // seq_count, out_weight.shape[1]), "seq", 0, 0, tiled=True
        ).astype(f32),
        axis=0,
    )
    own, *sent = head_call(
        project_kernel,
        "project",
        heads,
        [("whole", (tokens, features), f32)] + [("whole", (tokens, features), bf16)] * (parts - 1),
        ("scalar", head_place),
        ("whole", mixed),
        ("whole", out_weight),
        steps=1,
    )
    query_grad, key_grad, value_grad, logit_grad = head_call(
        gradient_kernel,
        "gradients",
        heads,
        [
            ("last", queries.shape, f32),
            ("last", keys.shape, f32),
            ("last", values.shape, f32),
            ("first", (heads, blocks, ROWS), f32),
        ],
        ("last", queries),
        ("last", keys),
        ("first", logit_rows),
        ("first", system),
        ("first", solved),
        ("first", step),
        ("first", states),
        ("first", drive),
        ("last", mixed_grad),
        ("first", after),
        ("first", behind),
        ("free", far_adjoint),
    )
    for mask, share in enumerate(sent, 1):
        own = own + exchanged(share, "head", mask).astype(f32)
    output = own.astype(bf16)
    logit_grad = logit_grad.reshape(heads, blocks, 2, BLOCK).transpose(2, 0, 1, 3).reshape(beta_logit.shape)
    return (
        output,
        query_grad,
        key_grad,
        value_grad,
        logit_grad,
        weight_grad,
    )


def solution(mesh):
    in_specs = (
        P("seq", "head"),
        P("seq", None, "head"),
        P("seq", None, "head"),
        P(None, "head", "seq"),
        P("head", None),
        P("seq", "head"),
    )
    out_specs = (
        P("seq", "head"),
        P("seq", "head"),
        P("seq", None, "head"),
        P("seq", None, "head"),
        P(None, "head", "seq"),
        P(("head", "seq"), None),
    )
    return jax.shard_map(body, mesh=mesh, in_specs=in_specs, out_specs=out_specs, check_vma=False)
```
